1024 devices in a mesh: rep: 8 (over x, core), node: 8 (over y), local: 16 (over z).
Axes of the slice: x: 4, y: 8, z: 16, core: 2. Of those that a mesh axis runs over, the one named last changes fastest.
Arguments:
- tokens: bfloat16 [2048, 3584], P(('rep', 'node', 'local')), may hold values from -6 to 6
- cotangent: bfloat16 [2048, 3584], P(('rep', 'node', 'local')), may hold values from -1.1953125 to 1.1953125
- expert_ids: int32 [2048, 8], P(('rep', 'node', 'local')), may hold values from 0 to 127, as said below
- node_groups: int32 [2048, 4], P(('rep', 'node', 'local')), may hold values from 0 to 7, as said below
- route_weight: bfloat16 [2048, 8], P(('rep', 'node', 'local')), may hold values from 0.099609375 to 1
- w_gate: bfloat16 [128, 3584, 1024], P(('node', 'local'), None, 'rep'), may hold values from -0.09375 to 0.09375
- w_up: bfloat16 [128, 3584, 1024], P(('node', 'local'), None, 'rep'), may hold values from -0.09375 to 0.09375
- w_down: bfloat16 [128, 1024, 3584], P(('node', 'local'), 'rep'), may hold values from -0.1875 to 0.1875
Outputs:
- mixed: bfloat16 [2048, 3584], P(('rep', 'node', 'local'))
- grad_x: bfloat16 [2048, 3584], P(('rep', 'node', 'local'))
- grad_route: bfloat16 [2048, 8], P(('rep', 'node', 'local'))
The draws below stay inside these ranges and needn't reach their ends.
Inputs may be any that keep to these rules, and one draw needn't show every extreme that they name: `expert_ids`: each row names 8 different experts: one or two in each node group that node_groups lists for the row, and at most one in each other node group. Counting only the picks whose node group the row lists, among the 16 rows of the devices that share one rep index and one local index, no expert is named by more than 2 rows, and in every node group some expert is named by exactly 2 of them. `node_groups`: each row lists 4 different node groups. Among the 16 rows of the devices that share one rep index and one local index, every node group is listed by exactly half of the rows.
All inputs are finite; a program needn't handle non-finite values.
Results may differ from the reference program's by a relative error of at most 0.03.
Values may be sent and summed in bfloat16 or wider, within the bound.
No kernel may reach another device: no remote copies, remote signals or barrier semaphores. Data moves between devices by JAX's collectives and lax.ppermute only.
A program may use at most 32 MiB of HBM per device.

```python
import math
import jax
import jax.numpy as jnp
from jax import lax

D = 3584
HID = 1024
TOK_DEV = 2
EXPERTS = 128
LIMIT = 4
TOP = 8
BLOCK = 16
CAP = 2
TOKENS = 2048
N_REP = 8
N_NODE = 8
N_LOCAL = 16


def distinct_scores(key, shape, span):
    raw_draw = jax.random.randint(key, shape, 0, 1 << 20, dtype=jnp.int32)
    return raw_draw * span + jnp.arange(span, dtype=jnp.int32)


def routing_tables(key):
    blocks = N_REP * N_LOCAL
    choosers = BLOCK // 2
    key_groups, key_rows, key_rank, key_local, key_moved = jax.random.split(key, 5)
    group_order = jnp.argsort(distinct_scores(key_groups, (blocks, N_NODE), N_NODE), axis=1, stable=True).astype(jnp.int32)
    row_order = jnp.argsort(distinct_scores(key_rows, (blocks, BLOCK), BLOCK), axis=1, stable=True)
    row_rank = jnp.argsort(row_order, axis=1, stable=True).astype(jnp.int32)
    offsets = (row_rank[:, :, None] % N_NODE + jnp.arange(LIMIT, dtype=jnp.int32)[None, None, :]) % N_NODE
    order_wide = jnp.broadcast_to(group_order[:, None, :], (blocks, BLOCK, N_NODE))
    row_groups = jnp.take_along_axis(order_wide, offsets, axis=2)
    partner_groups = jnp.take_along_axis(order_wide, (offsets + LIMIT) % N_NODE, axis=2)
    member = row_groups[:, :, :, None] == jnp.arange(N_NODE, dtype=jnp.int32)
    chooser = jnp.transpose(jnp.any(member, axis=2), (0, 2, 1))
    rank_scores = distinct_scores(key_rank, (blocks, N_NODE, BLOCK), BLOCK)
    ranked_below = (rank_scores[:, :, None, :] < rank_scores[:, :, :, None]) & chooser[:, :, None, :]
    chooser_rank = jnp.sum(ranked_below.astype(jnp.int32), axis=3).astype(jnp.int32)
    base_load = (BLOCK - CAP) // (N_LOCAL - 1)
    extra_load = (BLOCK - CAP) % (N_LOCAL - 1)
    local_range = jnp.arange(N_LOCAL, dtype=jnp.int32)
    load_sizes = jnp.where(local_range == 0, CAP, jnp.where(local_range <= extra_load, base_load + 1, base_load))
    bounds = jnp.cumsum(load_sizes).astype(jnp.int32)
    local_order = jnp.argsort(distinct_scores(key_local, (blocks, N_NODE, N_LOCAL), N_LOCAL), axis=2, stable=True).astype(jnp.int32)
    pick_list = []
    for second in range(2):
        position = chooser_rank + second * choosers
        segment = jnp.sum((bounds <= position[..., None]).astype(jnp.int32), axis=3)
        segment = jnp.minimum(segment, N_LOCAL - 1).astype(jnp.int32)
        pick_list.append(jnp.take_along_axis(local_order, segment, axis=2))
    locals_all = jnp.stack(pick_list, axis=-1)
    experts_all = jnp.arange(N_NODE, dtype=jnp.int32)[None, :, None, None] * N_LOCAL + locals_all
    experts_all = jnp.transpose(experts_all, (0, 2, 1, 3))
    chosen_ids = jnp.sum(jnp.where(member[..., None], experts_all[:, :, None, :, :], 0), axis=3).astype(jnp.int32)
    moved = jax.random.randint(key_moved, (blocks, BLOCK, LIMIT), 0, 4, dtype=jnp.int32) == 0
    second_ids = jnp.where(moved, partner_groups * N_LOCAL + chosen_ids[..., 1] % N_LOCAL, chosen_ids[..., 1])
    chosen_ids = jnp.stack([chosen_ids[..., 0], second_ids.astype(jnp.int32)], axis=-1)
    expert_table = chosen_ids.reshape(N_REP, N_LOCAL, N_NODE, TOK_DEV, TOP)
    expert_table = jnp.transpose(expert_table, (0, 2, 1, 3, 4)).reshape(TOKENS, TOP).astype(jnp.int32)
    groups = row_groups.reshape(N_REP, N_LOCAL, N_NODE, TOK_DEV, LIMIT)
    groups = jnp.transpose(groups, (0, 2, 1, 3, 4)).reshape(TOKENS, LIMIT).astype(jnp.int32)
    return (expert_table, groups)


def draw_expert_ids(key, part):
    return routing_tables(key)[0]


def draw_node_groups(key, part):
    return routing_tables(key)[1]


def block_scale(rng, dims, pieces, least, largest):
    factor_of = 1.0
    for dim, shards_of in pieces:
        heights = jax.random.uniform(jax.random.fold_in(jax.random.fold_in(rng, 6), dim), (shards_of,), jnp.float32, least / len(pieces), largest / len(pieces))
        factor_of = factor_of * jnp.repeat(jnp.exp(heights), dims[dim] // shards_of).reshape((-1,) + (1,) * (len(dims) - 1 - dim))
    return factor_of


def bell_draw(key, dims, scale, reach, cuts=(), kind=jnp.bfloat16):
    level = block_scale(key, dims, cuts, -0.22, 0.18) if cuts else 1.0
    drawn = jax.random.normal(key, dims, jnp.float32) * scale * level
    return jnp.minimum(jnp.maximum(drawn, -reach), reach).astype(kind)


def setup_inputs(seed: int = 0) -> dict:
    splits = jax.random.split(jax.random.key(seed), 9)
    tokens = bell_draw(splits[0], (TOKENS, D), 1.0, 6.0, ((0, 1024),))
    cotangent = bell_draw(splits[1], (TOKENS, D), 0.2, 1.1953125, ((0, 1024),))
    expert_ids = draw_expert_ids(jax.random.fold_in(splits[8], 71), 0)
    node_groups = draw_node_groups(jax.random.fold_in(splits[8], 71), 0)
    route_weight = jnp.clip(jnp.exp(math.log(1.0) - 2.306499 * jax.random.uniform(splits[4], (TOKENS, TOP), jnp.float32) ** block_scale(splits[4], (TOKENS, TOP), ((0, 1024),), -0.2, 0.2)), 0.099609375, 1.0).astype(jnp.bfloat16)
    w_gate = bell_draw(splits[5], (EXPERTS, D, HID), D ** -0.5, 0.09375, ((0, 128), (2, 8)))
    w_up = bell_draw(splits[6], (EXPERTS, D, HID), D ** -0.5, 0.09375, ((0, 128), (2, 8)))
    w_down = bell_draw(splits[7], (EXPERTS, HID, D), HID ** -0.5, 0.1875, ((0, 128), (1, 8)))
    return dict(tokens=tokens, cotangent=cotangent, expert_ids=expert_ids, node_groups=node_groups, route_weight=route_weight, w_gate=w_gate, w_up=w_up, w_down=w_down)


def slot_positions(expert_ids, node_groups):
    ids_grid = expert_ids.reshape(N_REP, N_NODE, N_LOCAL, TOK_DEV, TOP)
    group_grid = node_groups.reshape(N_REP, N_NODE, N_LOCAL, TOK_DEV, LIMIT)
    chosen = jnp.any((ids_grid // N_LOCAL)[..., None] == group_grid[..., None, :], axis=-1)
    ids_block = jnp.transpose(ids_grid, (0, 2, 1, 3, 4)).reshape(N_REP, N_LOCAL, BLOCK, TOP)
    chosen_block = jnp.transpose(chosen, (0, 2, 1, 3, 4)).reshape(N_REP, N_LOCAL, BLOCK, TOP)
    hits = (ids_block[..., None] == jnp.arange(EXPERTS, dtype=jnp.int32)) & chosen_block[..., None]
    per_row = jnp.sum(hits.astype(jnp.int32), axis=3).astype(jnp.int32)
    before = (jnp.cumsum(per_row, axis=2) - per_row).astype(jnp.int32)
    slot_block = jnp.sum(jnp.where(hits, before[:, :, :, None, :], 0), axis=4).astype(jnp.int32)
    replica = jnp.arange(N_REP, dtype=jnp.int32)[:, None, None, None]
    local_index = jnp.arange(N_LOCAL, dtype=jnp.int32)[None, :, None, None]
    total_slots = EXPERTS * N_REP * N_LOCAL * CAP
    position = ((ids_block * N_REP + replica) * N_LOCAL + local_index) * CAP + slot_block
    position = jnp.where(chosen_block, position, total_slots).astype(jnp.int32)
    position = jnp.transpose(position.reshape(N_REP, N_LOCAL, N_NODE, TOK_DEV, TOP), (0, 2, 1, 3, 4))
    return position.reshape(TOKENS, TOP).astype(jnp.int32), chosen.reshape(TOKENS, TOP)


def expert_pass(tokens_pad, cot_pad, weight_pad, gate_weight, up_weight, down_weight, picks):
    share = HID // N_REP
    row_index = (picks // TOP).astype(jnp.int32)
    slot_rows = tokens_pad[row_index]
    slot_cot = cot_pad[row_index]
    slot_count = slot_rows.shape[0]
    slot_scale = weight_pad[picks].astype(jnp.float32)[:, None]
    scaled_cot = (slot_scale * slot_cot.astype(jnp.float32)).astype(jnp.bfloat16)
    gate_pre = jnp.dot(slot_rows, gate_weight, preferred_element_type=jnp.float32)
    up_pre = jnp.dot(slot_rows, up_weight, preferred_element_type=jnp.float32)
    sigmoid_gate = jax.nn.sigmoid(gate_pre)
    active = gate_pre * sigmoid_gate
    hidden = (active * up_pre).astype(jnp.bfloat16)
    hidden_three = hidden.reshape(slot_count, N_REP, share).astype(jnp.float32)
    down_three = down_weight.reshape(N_REP, share, D).astype(jnp.float32)
    part_out = jnp.einsum("snh,nhd->nsd", hidden_three, down_three, precision=lax.Precision.HIGHEST)
    part_out = lax.optimization_barrier(part_out.astype(jnp.bfloat16))
    expert_out = jnp.sum(part_out.astype(jnp.float32), axis=0)
    route_grad = jnp.sum(slot_cot.astype(jnp.float32) * expert_out, axis=1).astype(jnp.bfloat16)
    grad_hidden = jnp.dot(scaled_cot, down_weight.T, preferred_element_type=jnp.float32)
    grad_gate_pre = (grad_hidden * up_pre * sigmoid_gate * (1.0 + gate_pre * (1.0 - sigmoid_gate))).astype(jnp.bfloat16)
    grad_up_pre = (grad_hidden * active).astype(jnp.bfloat16)
    gate_three = gate_weight.reshape(D, N_REP, share).astype(jnp.float32)
    up_three = up_weight.reshape(D, N_REP, share).astype(jnp.float32)
    part_gx = (jnp.einsum("snh,dnh->nsd", grad_gate_pre.reshape(slot_count, N_REP, share).astype(jnp.float32), gate_three,
                          precision=lax.Precision.HIGHEST)
               + jnp.einsum("snh,dnh->nsd", grad_up_pre.reshape(slot_count, N_REP, share).astype(jnp.float32), up_three,
                            precision=lax.Precision.HIGHEST))
    part_gx = lax.optimization_barrier(part_gx.astype(jnp.bfloat16))
    slot_grad_x = jnp.sum(part_gx.astype(jnp.float32), axis=0).astype(jnp.bfloat16)
    return expert_out.astype(jnp.bfloat16), slot_grad_x, route_grad


def reference(tokens, cotangent, expert_ids, node_groups, route_weight, w_gate, w_up, w_down):
    position, chosen = slot_positions(expert_ids, node_groups)
    total_slots = EXPERTS * N_REP * N_LOCAL * CAP
    pick_total = TOKENS * TOP
    table = jnp.full((total_slots + 1,), pick_total, dtype=jnp.int32)
    table = table.at[position.reshape(-1)].set(jnp.arange(pick_total, dtype=jnp.int32))
    table = table[:total_slots].reshape(EXPERTS, N_REP * N_LOCAL * CAP)
    tokens_pad = jnp.concatenate([tokens, jnp.zeros((1, D), jnp.bfloat16)], axis=0)
    cot_pad = jnp.concatenate([cotangent, jnp.zeros((1, D), jnp.bfloat16)], axis=0)
    weight_pad = jnp.concatenate([route_weight.reshape(-1), jnp.zeros((1,), jnp.bfloat16)], axis=0)

    def step(buffers, inputs):
        out_buf, grad_buf, route_buf = buffers
        gate_weight, up_weight, down_weight, picks = inputs
        out_rows, grad_rows, route_rows = expert_pass(tokens_pad, cot_pad, weight_pad, gate_weight, up_weight, down_weight, picks)
        return (out_buf.at[picks].set(out_rows), grad_buf.at[picks].set(grad_rows), route_buf.at[picks].set(route_rows)), None

    start_buffers = (jnp.zeros((pick_total + 1, D), jnp.bfloat16), jnp.zeros((pick_total + 1, D), jnp.bfloat16),
                     jnp.zeros((pick_total + 1,), jnp.bfloat16))
    (out_buf, grad_buf, route_buf), unused = lax.scan(step, start_buffers, (w_gate, w_up, w_down, table))

    rows_rep = TOKENS // N_REP
    pick_out = out_buf[:pick_total].reshape(N_REP, rows_rep, TOP, D)
    pick_grad = grad_buf[:pick_total].reshape(N_REP, rows_rep, TOP, D)
    weights_rep = route_weight.reshape(N_REP, rows_rep, TOP)
    groups_rep = (expert_ids // N_LOCAL).astype(jnp.int32).reshape(N_REP, rows_rep, TOP)
    chosen_rep = chosen.reshape(N_REP, rows_rep, TOP)

    def combine(args):
        outs, grads, weights, pick_groups, chosen_here = args
        outs_f = outs.astype(jnp.float32)
        grads_f = grads.astype(jnp.float32)
        mixed_sum = jnp.zeros((rows_rep, D), jnp.float32)
        grad_sum = jnp.zeros((rows_rep, D), jnp.float32)
        for group_index in range(N_NODE):
            inside = chosen_here & (pick_groups == group_index)
            scale = jnp.where(inside, weights.astype(jnp.float32), jnp.zeros((), jnp.float32))
            part_out = jnp.einsum("nk,nkd->nd", scale, outs_f, precision=lax.Precision.HIGHEST)
            part_out = lax.optimization_barrier(part_out.astype(jnp.bfloat16))
            mixed_sum = mixed_sum + part_out.astype(jnp.float32)
            part_grad = jnp.einsum("nk,nkd->nd", inside.astype(jnp.float32), grads_f, precision=lax.Precision.HIGHEST)
            part_grad = lax.optimization_barrier(part_grad.astype(jnp.bfloat16))
            grad_sum = grad_sum + part_grad.astype(jnp.float32)
        return mixed_sum.astype(jnp.bfloat16), grad_sum.astype(jnp.bfloat16)

    mixed, grad_x = lax.map(combine, (pick_out, pick_grad, weights_rep, groups_rep, chosen_rep))
    mixed = mixed.reshape(TOKENS, D)
    grad_x = grad_x.reshape(TOKENS, D)
    grad_route = jnp.where(chosen, route_buf[:pick_total].reshape(TOKENS, TOP), jnp.zeros((), jnp.bfloat16))
    return mixed, grad_x, grad_route
```

```python
import jax
import jax.numpy as jnp
import numpy as np
from jax import lax
from jax.sharding import Mesh, PartitionSpec as P

BF = jnp.bfloat16
F32 = jnp.float32


def dot(left_side, right_side, left_dim=1, right_dim=0):
    return lax.dot_general(
        left_side,
        right_side,
        (((left_dim,), (right_dim,)), ((), ())),
        preferred_element_type=F32,
    )


def local(tokens, cotangent, expert_ids, node_groups, route_weight, w_gate, w_up, w_down):
    node_count = lax.axis_size("node")
    local_count = lax.axis_size("local")
    tok_rows, width = tokens.shape
    top_count = expert_ids.shape[1]
    limit = node_groups.shape[1]
    rows = tok_rows * node_count
    capacity = 2 * rows // local_count
    slots = local_count * capacity
    swap = [(0, 1), (1, 0)]

    gates = (w_gate[0], lax.ppermute(w_gate[0], "core", swap))
    ups = (w_up[0], lax.ppermute(w_up[0], "core", swap))
    downs = (w_down[0], lax.ppermute(w_down[0], "core", swap))

    used = 2 * top_count + limit
    info = jnp.concatenate(
        [
            expert_ids.astype(BF),
            node_groups.astype(BF),
            route_weight,
            jnp.zeros((tok_rows, 128 - used), BF),
        ],
        axis=1,
    )
    payload = jnp.concatenate([tokens, cotangent, info], axis=1)
    gathered = lax.all_gather(payload, "node", axis=0, tiled=True)
    tok = gathered[:, :width]
    cot = gathered[:, width : 2 * width]
    info = gathered[:, 2 * width :].astype(F32)
    ids = info[:, :top_count].astype(jnp.int32)
    groups = info[:, top_count : top_count + limit].astype(jnp.int32)
    weights = info[:, top_count + limit : used]

    me = lax.axis_index("node")
    listed = jnp.any(groups == me, axis=1)
    mine = (ids // local_count == me) & listed[:, None]
    expert_range = jnp.arange(local_count, dtype=jnp.int32)
    pick_hit = mine[:, None, :] & ((ids % local_count)[:, None, :] == expert_range[None, :, None])
    hit = jnp.any(pick_hit, axis=2)
    weight_of = jnp.sum(jnp.where(pick_hit, weights[:, None, :], 0.0), axis=2)
    hit_i = hit.astype(jnp.int32)
    before = jnp.cumsum(hit_i, axis=0) - hit_i
    slot_range = jnp.arange(capacity, dtype=jnp.int32)
    place = hit[:, :, None] & (before[:, :, None] == slot_range)
    place_f = place.astype(F32)
    place_w = (place_f * weight_of[:, :, None]).astype(BF).reshape(rows, slots)
    place_b = place_f.astype(BF).reshape(rows, slots)
    send_tok = dot(place_b, tok, 0, 0).astype(BF)
    send_cot = dot(place_w, cot, 0, 0).astype(BF)

    got_tok = lax.all_to_all(send_tok, "local", split_axis=0, concat_axis=0, tiled=True)
    got_cot = lax.all_to_all(send_cot, "local", split_axis=0, concat_axis=0, tiled=True)
    all_tok = lax.all_gather(got_tok, "x", axis=0, tiled=True)
    all_cot = lax.all_gather(got_cot, "x", axis=0, tiled=True)

    part_out = 0.0
    kept = []
    for gate_w, up_w, down_w in zip(gates, ups, downs):
        gate_pre = dot(all_tok, gate_w)
        up_pre = dot(all_tok, up_w)
        sig = jax.nn.sigmoid(gate_pre)
        active = gate_pre * sig
        hidden = (active * up_pre).astype(BF)
        part_out = part_out + dot(hidden, down_w)
        kept.append((gate_pre, up_pre, sig, active))
    out_parts = lax.all_to_all(part_out.astype(BF), "x", split_axis=0, concat_axis=0, tiled=True)

    part_gx = 0.0
    for gate_w, up_w, down_w, (gate_pre, up_pre, sig, active) in zip(gates, ups, downs, kept):
        grad_hidden = dot(all_cot, down_w, 1, 1)
        grad_gate = (grad_hidden * up_pre * sig * (1.0 + gate_pre * (1.0 - sig))).astype(BF)
        grad_up = (grad_hidden * active).astype(BF)
        part_gx = part_gx + dot(grad_gate, gate_w, 1, 1) + dot(grad_up, up_w, 1, 1)
    gx_parts = lax.all_to_all(part_gx.astype(BF), "x", split_axis=0, concat_axis=0, tiled=True)

    def reduce_parts(parts):
        return jnp.sum(parts.reshape(-1, slots, width).astype(F32), axis=0).astype(BF)

    back_out = lax.all_to_all(
        reduce_parts(out_parts), "local", split_axis=0, concat_axis=0, tiled=True
    )
    back_gx = lax.all_to_all(
        reduce_parts(gx_parts), "local", split_axis=0, concat_axis=0, tiled=True
    )

    group_out = dot(place_w, back_out).astype(BF)
    pair_sum = dot(cot, back_out, 1, 1).reshape(rows, local_count, capacity)
    slot_route = jnp.sum(pair_sum * place_f, axis=2)
    route = jnp.sum(jnp.where(pick_hit, slot_route[:, :, None], 0.0), axis=1).astype(BF)
    route = jnp.concatenate([route, jnp.zeros((rows, 128 - top_count), BF)], axis=1)
    home_out = lax.all_to_all(
        jnp.concatenate([group_out, route], axis=1),
        "node",
        split_axis=0,
        concat_axis=0,
        tiled=True,
    )
    group_gx = dot(place_b, back_gx).astype(BF)
    home_gx = lax.all_to_all(group_gx, "node", split_axis=0, concat_axis=0, tiled=True)
    home = jnp.sum(home_out.reshape(node_count, tok_rows, -1).astype(F32), axis=0).astype(BF)
    mixed = home[:, :width]
    grad_route = home[:, width : width + top_count]
    grad_x = jnp.sum(home_gx.reshape(node_count, tok_rows, width).astype(F32), axis=0).astype(BF)
    return (mixed, grad_x, grad_route)


def solution(mesh):
    shape = mesh.devices.shape
    split = Mesh(
        np.asarray(mesh.devices).reshape((shape[0] // 2, 2) + shape[1:]),
        ("x", "core", "node", "local"),
    )
    row_spec = P(("x", "core", "node", "local"), None)
    return jax.shard_map(
        local,
        mesh=split,
        in_specs=(
            row_spec,
            row_spec,
            row_spec,
            row_spec,
            row_spec,
            P(("node", "local"), None, ("x", "core")),
            P(("node", "local"), None, ("x", "core")),
            P(("node", "local"), ("x", "core"), None),
        ),
        out_specs=(row_spec, row_spec, row_spec),
        check_vma=False,
    )
```

```python
import functools

import jax
import jax.numpy as jnp
import numpy as np
from jax import lax
from jax.experimental import pallas as pl
from jax.experimental.pallas import tpu as pltpu
from jax.sharding import Mesh, PartitionSpec as P


BF = jnp.bfloat16
F32 = jnp.float32
LANES = 128
VMEM = pl.BlockSpec(memory_space=pltpu.VMEM)
MIB = 1024 * 1024


def dot(left_side, right_side, left_dim=1, right_dim=0):
    return lax.dot_general(
        left_side,
        right_side,
        (((left_dim,), (right_dim,)), ((), ())),
        preferred_element_type=F32,
    )


def iota(shape, dim):
    return lax.broadcasted_iota(jnp.int32, shape, dim)


def payload_kernel(tok_ref, cot_ref, ids_ref, groups_ref, weight_ref, out_ref, block_ref):
    tok_rows, width = tok_ref.shape
    half = width // 2
    lane = iota((tok_rows, LANES), 1)
    info = jnp.zeros((tok_rows, LANES), F32)
    place = 0
    for ref in (ids_ref, groups_ref, weight_ref):
        values = ref[...].astype(F32)
        for k in range(values.shape[1]):
            info = info + jnp.where(lane == place, values[:, k : k + 1], 0.0)
            place += 1
    for h in range(2):
        for kind, ref in enumerate((tok_ref, cot_ref)):
            at = pl.ds((2 * h + kind) * tok_rows, tok_rows)
            block_ref[at, :half] = ref[:, h * half : (h + 1) * half].astype(F32)
            block_ref[at, half:] = info
    block = block_ref[...].astype(BF)
    size = block.shape[0]
    for y in range(out_ref.shape[0] // size):
        out_ref[y * size : (y + 1) * size, :] = block


def routing(info, me, top_count, limit, local_count):
    shape = (info.shape[0], 8 * local_count)
    col = iota(shape, 1)
    row = iota(shape, 0)
    target = (me * local_count + (col >> 3)).astype(F32)
    listed = jnp.zeros((info.shape[0], 1), F32)
    for j in range(limit):
        match = info[:, top_count + j : top_count + j + 1] == me.astype(F32)
        listed = jnp.maximum(listed, match.astype(F32))
    first_weight = top_count + limit
    hit = jnp.zeros(shape, F32)
    weight = jnp.zeros(shape, F32)
    picks = []
    for k in range(top_count):
        match = (info[:, k : k + 1] == target).astype(F32) * listed
        picks.append(match)
        hit = hit + match
        weight = weight + match * info[:, first_weight + k : first_weight + k + 1]
    return row, col, hit, weight, picks


def placed(hit, row, col, kind):
    rows = hit.shape[0]
    mine = (((row >> 1) & 1) == kind) & (((row >> 2) & 1) == ((col >> 2) & 1))
    hit = jnp.where(mine, hit, 0.0)
    earlier = (iota((rows, rows), 1) < iota((rows, rows), 0)).astype(F32).astype(BF)
    before = dot(earlier, hit.astype(BF))
    return jnp.where(before == (col & 1).astype(F32), hit, 0.0)


def side(place, col, p):
    return jnp.where(((col >> 1) & 1) == p, place, 0.0).astype(BF)


def dispatch_kernel(top_count, limit, local_count, me_ref, rows_ref, tok_ref, cot_ref):
    quarter = tok_ref.shape[1]
    info = rows_ref[:, 2 * quarter :].astype(F32)
    row, col, hit, weight, _ = routing(info, me_ref[0], top_count, limit, local_count)
    for kind, out_ref in enumerate((tok_ref, cot_ref)):
        place = placed(hit, row, col, kind)
        if kind == 1:
            place = place * weight
        out_ref[...] = sum(
            dot(side(place, col, p), rows_ref[:, p * quarter : (p + 1) * quarter], 0, 0)
            for p in range(2)
        ).astype(BF)


def plain_order(local_count):
    size = 8 * local_count
    i = iota((size, size), 0)
    quarter = i // (2 * local_count)
    rest = i % (2 * local_count)
    where = (rest >> 1) * 8 + quarter * 2 + (rest & 1)
    return (where == iota((size, size), 1)).astype(F32).astype(BF)


def quarters(local_count, refs):
    order = plain_order(local_count)
    slots = 2 * local_count
    blocks = [dot(order, ref[...]).astype(BF) for ref in refs]
    return [
        jnp.concatenate([block[q * slots : (q + 1) * slots] for block in blocks], axis=0)
        for q in range(4)
    ]


def put_parts(q, value, my_ref, their_refs):
    slots = value.shape[0] // (1 + len(their_refs))
    at = pl.ds(q * slots, slots)
    my_ref[at, :] = value[:slots]
    for b, ref in enumerate(their_refs):
        ref[at, :] = value[(b + 1) * slots : (b + 2) * slots].astype(BF)


def forward_kernel(local_count, *refs):
    rows, weights = refs[:4], refs[4:10]
    outs = refs[10:14]
    slope_ref, active_ref = refs[14:16]
    quarter = rows[0].shape[1]
    tok = quarters(local_count, rows)
    part = slope_ref.shape[1] // 2
    hidden = []
    for c in range(2):
        gate_ref, up_ref, _ = weights[3 * c : 3 * c + 3]
        gate_pre = up_pre = 0.0
        for q in range(4):
            at = pl.ds(q * quarter, quarter)
            gate_pre = gate_pre + dot(tok[q], gate_ref[at, :])
            up_pre = up_pre + dot(tok[q], up_ref[at, :])
        sig = 1.0 / (1.0 + jnp.exp(-gate_pre))
        active = gate_pre * sig
        hidden.append((active * up_pre).astype(BF))
        cols = pl.ds(c * part, part)
        slope_ref[:, cols] = up_pre * sig * (1.0 + gate_pre * (1.0 - sig))
        active_ref[:, cols] = active
    for q in range(4):
        cols = pl.ds(q * quarter, quarter)
        value = dot(hidden[0], weights[2][:, cols]) + dot(hidden[1], weights[5][:, cols])
        put_parts(q, value, outs[0], outs[1:])


def backward_kernel(local_count, *refs):
    rows, slope_ref, active_ref = refs[:4], refs[4], refs[5]
    weights, outs = refs[6:12], refs[12:16]
    quarter = rows[0].shape[1]
    cot = quarters(local_count, rows)
    part = slope_ref.shape[1] // 2
    grads = []
    for c in range(2):
        down_ref = weights[3 * c + 2]
        grad_hidden = 0.0
        for q in range(4):
            grad_hidden = grad_hidden + dot(cot[q], down_ref[:, q * quarter : (q + 1) * quarter], 1, 1)
        cols = pl.ds(c * part, part)
        grads.append((grad_hidden * slope_ref[:, cols]).astype(BF))
        grads.append((grad_hidden * active_ref[:, cols]).astype(BF))
    for q in range(4):
        at = pl.ds(q * quarter, quarter)
        value = 0.0
        for c in range(2):
            value = value + dot(grads[2 * c], weights[3 * c][at, :], 1, 1)
            value = value + dot(grads[2 * c + 1], weights[3 * c + 1][at, :], 1, 1)
        put_parts(q, value, outs[0], outs[1:])


def total_kernel(local_count, my_ref, *refs):
    total = my_ref[...]
    for ref in refs[:-1]:
        total = total + ref[...].astype(F32)
    refs[-1][...] = dot(plain_order(local_count), total.astype(BF), 0, 0).astype(BF)


def combine_kernel(top_count, limit, local_count, me_ref, rows_ref, out_back, grad_back, out_ref):
    quarter = out_back.shape[1]
    info = rows_ref[:, 2 * quarter :].astype(F32)
    row, col, hit, weight, picks = routing(info, me_ref[0], top_count, limit, local_count)
    place_out = placed(hit, row, col, 0) * weight
    place_grad = placed(hit, row, col, 1)
    pair_sum = 0.0
    for p in range(2):
        cols = pl.ds(p * quarter, quarter)
        grad_side = side(place_grad, col, p)
        value = dot(side(place_out, col, p), out_back[...]) + dot(grad_side, grad_back[...])
        out_ref[:, cols] = value.astype(BF)
        pair_sum = pair_sum + dot(rows_ref[:, cols], out_back[...], 1, 1) * grad_side.astype(F32)
    lane = iota((info.shape[0], LANES), 1)
    route = jnp.zeros((info.shape[0], LANES), F32)
    for k in range(top_count):
        value = jnp.sum(pair_sum * picks[k], axis=1, keepdims=True)
        route = route + jnp.where(lane == k, value, 0.0)
    out_ref[:, 2 * quarter :] = route.astype(BF)


def home_kernel(rows_ref, mixed_ref, grad_ref, route_ref, sum_ref):
    tok_rows, width = mixed_ref.shape
    half = width // 2
    size = 4 * tok_rows
    rows = rows_ref[...].astype(F32)
    total = rows[:size]
    for y in range(1, rows_ref.shape[0] // size):
        total = total + rows[y * size : (y + 1) * size]
    sum_ref[...] = total
    for h in range(2):
        cols = slice(h * half, (h + 1) * half)
        first = 2 * h * tok_rows
        mixed_ref[:, cols] = sum_ref[first : first + tok_rows, :half].astype(BF)
        grad_ref[:, cols] = sum_ref[first + tok_rows : first + 2 * tok_rows, :half].astype(BF)
    info = sum_ref[tok_rows : 2 * tok_rows, half:] + sum_ref[3 * tok_rows : 4 * tok_rows, half:]
    route_ref[...] = info[:, : route_ref.shape[1]].astype(BF)


def exchange(array, axis):
    return lax.all_to_all(array, axis, split_axis=0, concat_axis=0, tiled=True)


def call(kernel, outs, name, *args, scratch=(), smem=0, vmem=8, flops=0):
    single = isinstance(outs, jax.ShapeDtypeStruct)
    arrays = args + ((outs,) if single else outs)
    cost = pl.CostEstimate(
        flops=flops,
        bytes_accessed=sum(a.size * a.dtype.itemsize for a in arrays),
        transcendentals=0,
    )
    return pl.pallas_call(
        kernel,
        out_shape=outs,
        in_specs=[pl.BlockSpec(memory_space=pltpu.SMEM)] * smem + [VMEM] * (len(args) - smem),
        out_specs=VMEM if single else (VMEM,) * len(outs),
        scratch_shapes=scratch,
        compiler_params=pltpu.CompilerParams(vmem_limit_bytes=vmem * MIB),
        cost_estimate=cost,
        name=name,
    )(*args)


def after(array, earlier):
    return lax.optimization_barrier((array, earlier))[0]


def local(tokens, cotangent, expert_ids, node_groups, route_weight, w_gate, w_up, w_down):
    x_count = lax.axis_size("x")
    node_count = lax.axis_size("node")
    local_count = lax.axis_size("local")
    tok_rows, width = tokens.shape
    top_count = expert_ids.shape[1]
    limit = node_groups.shape[1]
    half, quarter = width // 2, width // 4
    hid_part = w_gate.shape[2]
    node_rows = 4 * tok_rows * node_count
    swap = [(0, 1), (1, 0)]
    me = lax.axis_index("node").reshape(1).astype(jnp.int32)
    sizes = (top_count, limit, local_count)

    def shape(rows, cols, dtype=BF):
        return jax.ShapeDtypeStruct((rows, cols), dtype)

    slot_shape = shape(8 * local_count, quarter)
    slot_shape_f = shape(8 * local_count, quarter, F32)
    node_shape = shape(node_rows, half + LANES)
    block_scratch = [pltpu.VMEM((4 * tok_rows, half + LANES), F32)]
    kept_shape = shape(2 * local_count * x_count, 2 * hid_part, F32)

    def spread(array):
        return [
            lax.ppermute(array, "x", [(i, (i + k) % x_count) for i in range(x_count)])
            for k in range(1, x_count)
        ]

    def give_back(arrays):
        return [
            lax.ppermute(array, "x", [(i, (i - k) % x_count) for i in range(x_count)])
            for k, array in enumerate(arrays, 1)
        ]

    payload = call(
        payload_kernel,
        node_shape,
        "payload",
        tokens,
        cotangent,
        expert_ids,
        node_groups,
        route_weight,
        scratch=block_scratch,
        vmem=56,
    )
    gathered = exchange(payload, "node")
    send_tok, send_cot = call(
        functools.partial(dispatch_kernel, *sizes),
        (slot_shape, slot_shape),
        "dispatch",
        me,
        gathered,
        smem=1,
        vmem=44,
    )

    own = [w_gate[0], w_up[0], w_down[0]]
    weights = own + [lax.ppermute(w, "core", swap) for w in own]

    tok = exchange(send_tok, "local")
    cot = exchange(send_cot, "local")
    toks = [tok] + spread(tok)
    cots = [cot] + spread(cot)
    toks[0] = after(toks[0], cot)
    my_out, *their_out, slope, active = call(
        functools.partial(forward_kernel, local_count),
        (slot_shape_f, slot_shape, slot_shape, slot_shape, kept_shape, kept_shape),
        "forward",
        *toks,
        *weights,
        vmem=24,
        flops=12 * kept_shape.size * width // 2,
    )
    out_parts = give_back(their_out)
    my_grad, *their_grad = call(
        functools.partial(backward_kernel, local_count),
        (slot_shape_f, slot_shape, slot_shape, slot_shape),
        "backward",
        *cots,
        slope,
        active,
        *weights,
        vmem=24,
        flops=12 * kept_shape.size * width // 2,
    )
    grad_parts = give_back(their_grad)
    my_out = after(my_out, my_grad)
    total = functools.partial(total_kernel, local_count)
    total_out = call(total, slot_shape, "total_out", my_out, *out_parts)
    out_back = exchange(total_out, "local")
    my_grad = after(my_grad, out_back)
    total_grad = call(total, slot_shape, "total_grad", my_grad, *grad_parts)
    grad_back = exchange(total_grad, "local")
    combined = call(
        functools.partial(combine_kernel, *sizes),
        node_shape,
        "combine",
        me,
        gathered,
        out_back,
        grad_back,
        smem=1,
    )
    home = exchange(combined, "node")
    return call(
        home_kernel,
        (shape(tok_rows, width), shape(tok_rows, width), shape(tok_rows, top_count)),
        "home",
        home,
        scratch=block_scratch,
    )


def solution(mesh):
    shape = mesh.devices.shape
    split = Mesh(
        np.asarray(mesh.devices).reshape((shape[0] // 2, 2) + shape[1:]),
        ("x", "core", "node", "local"),
    )
    row_spec = P(("x", "core", "node", "local"), None)
    return jax.shard_map(
        local,
        mesh=split,
        in_specs=(
            row_spec,
            row_spec,
            row_spec,
            row_spec,
            row_spec,
            P(("node", "local"), None, ("x", "core")),
            P(("node", "local"), None, ("x", "core")),
            P(("node", "local"), ("x", "core"), None),
        ),
        out_specs=(row_spec, row_spec, row_spec),
        check_vma=False,
    )
```

```python
import functools

import jax
import jax.numpy as jnp
import numpy as np
from jax import lax
from jax.experimental import pallas as pl
from jax.experimental.pallas import tpu as pltpu
from jax.sharding import Mesh, PartitionSpec as P


BF = jnp.bfloat16
F32 = jnp.float32
LANES = 128
VMEM = pl.BlockSpec(memory_space=pltpu.VMEM)
MIB = 1024 * 1024


def dot(left_side, right_side, left_dim=1, right_dim=0):
    return lax.dot_general(
        left_side,
        right_side,
        (((left_dim,), (right_dim,)), ((), ())),
        preferred_element_type=F32,
    )


def iota(shape, dim):
    return lax.broadcasted_iota(jnp.int32, shape, dim)


def payload_kernel(tok_ref, cot_ref, ids_ref, groups_ref, weight_ref, out_ref, block_ref):
    tok_rows, width = tok_ref.shape
    half = width // 2
    lane = iota((tok_rows, LANES), 1)
    info = jnp.zeros((tok_rows, LANES), F32)
    place = 0
    for ref in (ids_ref, groups_ref, weight_ref):
        values = ref[...].astype(F32)
        for k in range(values.shape[1]):
            info = info + jnp.where(lane == place, values[:, k : k + 1], 0.0)
            place += 1
    for h in range(2):
        for kind, ref in enumerate((tok_ref, cot_ref)):
            at = pl.ds((2 * h + kind) * tok_rows, tok_rows)
            block_ref[at, :half] = ref[:, h * half : (h + 1) * half].astype(F32)
            block_ref[at, half:] = info
    block = block_ref[...].astype(BF)
    size = block.shape[0]
    for y in range(out_ref.shape[0] // size):
        out_ref[y * size : (y + 1) * size, :] = block


def routing(info, me, top_count, limit, local_count):
    shape = (info.shape[0], 8 * local_count)
    col = iota(shape, 1)
    row = iota(shape, 0)
    target = (me * local_count + (col >> 3)).astype(F32)
    listed = jnp.zeros((info.shape[0], 1), F32)
    for j in range(limit):
        match = info[:, top_count + j : top_count + j + 1] == me.astype(F32)
        listed = jnp.maximum(listed, match.astype(F32))
    first_weight = top_count + limit
    hit = jnp.zeros(shape, F32)
    weight = jnp.zeros(shape, F32)
    picks = []
    for k in range(top_count):
        match = (info[:, k : k + 1] == target).astype(F32) * listed
        picks.append(match)
        hit = hit + match
        weight = weight + match * info[:, first_weight + k : first_weight + k + 1]
    return row, col, hit, weight, picks


def placed(hit, col):
    rows = hit.shape[0]
    earlier = (iota((rows, rows), 1) < iota((rows, rows), 0)).astype(F32).astype(BF)
    before = dot(earlier, hit.astype(BF))
    return jnp.where(before == (col & 1).astype(F32), hit, 0.0)


def dispatch_kernel(top_count, limit, local_count, me_ref, rows_ref, out_ref):
    half = out_ref.shape[1]
    info = rows_ref[:, half:].astype(F32)
    row, col, hit, weight, _ = routing(info, me_ref[0], top_count, limit, local_count)
    same = ((row >> 1) & 3) == ((col >> 1) & 3)
    place = placed(jnp.where(same, hit, 0.0), col)
    scatter = jnp.where(((col >> 1) & 1) == 1, place * weight, place).astype(BF)
    out_ref[...] = dot(scatter, rows_ref[:, :half], 0, 0).astype(BF)


def plain_order(local_count):
    size = 8 * local_count
    i = iota((size, size), 0)
    quarter = i // (2 * local_count)
    rest = i % (2 * local_count)
    where = (rest >> 1) * 8 + quarter * 2 + (rest & 1)
    return (where == iota((size, size), 1)).astype(F32).astype(BF)


def join_kernel(*refs):
    gate_up, down = refs[6:]
    part = refs[0].shape[1]
    for c in range(2):
        for kind in range(2):
            gate_up[:, pl.ds((2 * kind + c) * part, part)] = refs[3 * c + kind][...]
        down[pl.ds(c * part, part), :] = refs[3 * c + 2][...]


def expert_kernel(local_count, blocks, *refs):
    rows, outs = refs[:blocks], refs[blocks + 2 :]
    gate_up, down = refs[blocks : blocks + 2]
    slots = 2 * local_count
    half = rows[0].shape[1]
    hidden_size = down.shape[0]
    order = plain_order(local_count)
    plain = [dot(order, ref[...]).astype(BF) for ref in rows]

    def every(h, kind):
        first = (2 * h + kind) * slots
        return jnp.concatenate([block[first : first + slots] for block in plain], axis=0)

    pre = dot(every(0, 0), gate_up[:half, :]) + dot(every(1, 0), gate_up[half:, :])
    gate_pre, up_pre = pre[:, :hidden_size], pre[:, hidden_size:]
    sig = 1.0 / (1.0 + jnp.exp(-gate_pre))
    active = gate_pre * sig
    hidden = (active * up_pre).astype(BF)
    grad_hidden = dot(every(0, 1), down[:, :half], 1, 1) + dot(every(1, 1), down[:, half:], 1, 1)
    grad_gate = (grad_hidden * up_pre * sig * (1.0 + gate_pre * (1.0 - sig))).astype(BF)
    grad_up = (grad_hidden * active).astype(BF)
    grads = jnp.concatenate([grad_gate, grad_up], axis=1)
    for h in range(2):
        cols = pl.ds(h * half, half)
        for kind, value in enumerate((dot(hidden, down[:, cols]), dot(grads, gate_up[cols, :], 1, 1))):
            at = pl.ds((2 * h + kind) * slots, slots)
            for b, ref in enumerate(outs):
                ref[at, :] = value[b * slots : (b + 1) * slots].astype(ref.dtype)


def near_sum_kernel(*refs):
    refs[-1][...] = sum(ref[...].astype(F32) for ref in refs[:-1])


def total_kernel(local_count, *refs):
    total = sum(ref[...].astype(F32) for ref in refs[:-1]).astype(BF)
    refs[-1][...] = dot(plain_order(local_count), total, 0, 0).astype(BF)


def combine_kernel(top_count, limit, local_count, me_ref, rows_ref, back_ref, out_ref):
    half = back_ref.shape[1]
    info = rows_ref[:, half:].astype(F32)
    row, col, hit, weight, picks = routing(info, me_ref[0], top_count, limit, local_count)
    same = ((row >> 1) & 3) == ((col >> 1) & 3)
    place = placed(jnp.where(same, hit, 0.0), col)
    gather = jnp.where(((col >> 1) & 1) == 0, place * weight, place).astype(BF)
    out_ref[:, :half] = dot(gather, back_ref[...]).astype(BF)
    crossed = (((row >> 1) & 3) == ((col >> 1) & 3) + 1) & (((row >> 1) & 1) == 1)
    place = placed(jnp.where(crossed, hit, 0.0), col)
    pair_sum = dot(rows_ref[:, :half], back_ref[...], 1, 1) * place
    lane = iota((info.shape[0], LANES), 1)
    route = jnp.zeros((info.shape[0], LANES), F32)
    for k in range(top_count):
        value = jnp.sum(pair_sum * picks[k], axis=1, keepdims=True)
        route = route + jnp.where(lane == k, value, 0.0)
    out_ref[:, half:] = route.astype(BF)


def home_kernel(rows_ref, mixed_ref, grad_ref, route_ref, sum_ref):
    tok_rows, width = mixed_ref.shape
    half = width // 2
    size = 4 * tok_rows
    rows = rows_ref[...].astype(F32)
    total = rows[:size]
    for y in range(1, rows_ref.shape[0] // size):
        total = total + rows[y * size : (y + 1) * size]
    sum_ref[...] = total
    for h in range(2):
        cols = slice(h * half, (h + 1) * half)
        first = 2 * h * tok_rows
        mixed_ref[:, cols] = sum_ref[first : first + tok_rows, :half].astype(BF)
        grad_ref[:, cols] = sum_ref[first + tok_rows : first + 2 * tok_rows, :half].astype(BF)
    info = sum_ref[tok_rows : 2 * tok_rows, half:] + sum_ref[3 * tok_rows : 4 * tok_rows, half:]
    route_ref[...] = info[:, : route_ref.shape[1]].astype(BF)


def exchange(array, axis):
    return lax.all_to_all(array, axis, split_axis=0, concat_axis=0, tiled=True)


def after(array, earlier):
    return lax.optimization_barrier((array, earlier))[0]


def call(kernel, outs, name, *args, scratch=(), smem=0, vmem=8, flops=0):
    single = isinstance(outs, jax.ShapeDtypeStruct)
    arrays = args + ((outs,) if single else outs)
    cost = pl.CostEstimate(
        flops=flops,
        bytes_accessed=sum(a.size * a.dtype.itemsize for a in arrays),
        transcendentals=0,
    )
    return pl.pallas_call(
        kernel,
        out_shape=outs,
        in_specs=[pl.BlockSpec(memory_space=pltpu.SMEM)] * smem + [VMEM] * (len(args) - smem),
        out_specs=VMEM if single else (VMEM,) * len(outs),
        scratch_shapes=scratch,
        compiler_params=pltpu.CompilerParams(vmem_limit_bytes=vmem * MIB),
        cost_estimate=cost,
        name=name,
    )(*args)


def local(tokens, cotangent, expert_ids, node_groups, route_weight, w_gate, w_up, w_down):
    x_count = lax.axis_size("x")
    node_count = lax.axis_size("node")
    local_count = lax.axis_size("local")
    tok_rows, width = tokens.shape
    top_count = expert_ids.shape[1]
    limit = node_groups.shape[1]
    half = width // 2
    hid_part = w_gate.shape[2]
    node_rows = 4 * tok_rows * node_count
    swap = [(0, 1), (1, 0)]
    me = lax.axis_index("node").reshape(1).astype(jnp.int32)
    sizes = (top_count, limit, local_count)

    def shape(rows, cols, dtype=BF):
        return jax.ShapeDtypeStruct((rows, cols), dtype)

    slot_shape = shape(8 * local_count, half)
    node_shape = shape(node_rows, half + LANES)
    block_scratch = [pltpu.VMEM((4 * tok_rows, half + LANES), F32)]

    def turn(array, k):
        return lax.ppermute(array, "x", [(i, (i + k) % x_count) for i in range(x_count)])

    payload = call(
        payload_kernel,
        node_shape,
        "payload",
        tokens,
        cotangent,
        expert_ids,
        node_groups,
        route_weight,
        scratch=block_scratch,
        vmem=56,
    )
    gathered = exchange(payload, "node")
    send = call(
        functools.partial(dispatch_kernel, *sizes), slot_shape, "dispatch", me, gathered, smem=1, vmem=44
    )

    own = [w_gate[0], w_up[0], w_down[0]]
    joined = call(
        join_kernel,
        (shape(width, 4 * hid_part), shape(2 * hid_part, width)),
        "join",
        *own,
        *[lax.ppermute(w, "core", swap) for w in own],
        vmem=20,
    )

    mine = after(exchange(send, "local"), joined[0])

    def experts(name, dtype, *blocks):
        return call(
            functools.partial(expert_kernel, local_count, len(blocks)),
            tuple(shape(*block.shape, dtype) for block in blocks),
            name,
            *blocks,
            *joined,
            vmem=16,
            flops=12 * len(blocks) * 2 * local_count * width * 2 * hid_part,
        )

    others = {k: turn(mine, k) for k in range(1, x_count)}
    (my_part,) = experts("mine", F32, mine)
    near = [k for k in others if k in (1, x_count - 1)]
    far = [k for k in others if k not in near]
    results = {}
    last = my_part
    for name, group in (("near", near), ("far", far)):
        if group:
            first, *rest = [others[k] for k in group]
            done = experts(name, BF, after(first, last), *rest)
            last = done[0]
            results[name] = [turn(part, -k) for k, part in zip(group, done)]
    near_sum = call(
        near_sum_kernel, shape(8 * local_count, half, F32), "near_sum", my_part, *results["near"]
    )
    total = call(
        functools.partial(total_kernel, local_count),
        slot_shape,
        "total",
        near_sum,
        *results.get("far", []),
    )
    back = exchange(total, "local")
    combined = call(
        functools.partial(combine_kernel, *sizes), node_shape, "combine", me, gathered, back, smem=1
    )
    home = exchange(combined, "node")
    return call(
        home_kernel,
        (shape(tok_rows, width), shape(tok_rows, width), shape(tok_rows, top_count)),
        "home",
        home,
        scratch=block_scratch,
    )


def solution(mesh):
    shape = mesh.devices.shape
    split = Mesh(
        np.asarray(mesh.devices).reshape((shape[0] // 2, 2) + shape[1:]),
        ("x", "core", "node", "local"),
    )
    row_spec = P(("x", "core", "node", "local"), None)
    return jax.shard_map(
        local,
        mesh=split,
        in_specs=(
            row_spec,
            row_spec,
            row_spec,
            row_spec,
            row_spec,
            P(("node", "local"), None, ("x", "core")),
            P(("node", "local"), None, ("x", "core")),
            P(("node", "local"), ("x", "core"), None),
        ),
        out_specs=(row_spec, row_spec, row_spec),
        check_vma=False,
    )
```

```python
import functools

import jax
import jax.numpy as jnp
import numpy as np
from jax import lax
from jax.experimental import pallas as pl
from jax.experimental.pallas import tpu as pltpu
from jax.sharding import Mesh, PartitionSpec as P


BF = jnp.bfloat16
F32 = jnp.float32
LANES = 128
VMEM = pl.BlockSpec(memory_space=pltpu.VMEM)
MIB = 1024 * 1024


def dot(left_side, right_side, left_dim=1, right_dim=0):
    return lax.dot_general(
        left_side,
        right_side,
        (((left_dim,), (right_dim,)), ((), ())),
        preferred_element_type=F32,
    )


def iota(shape, dim):
    return lax.broadcasted_iota(jnp.int32, shape, dim)


def payload_kernel(tok_ref, cot_ref, ids_ref, groups_ref, weight_ref, out_ref, block_ref):
    tok_rows, width = tok_ref.shape
    half = width // 2
    lane = iota((tok_rows, LANES), 1)
    info = jnp.zeros((tok_rows, LANES), F32)
    place = 0
    for ref in (ids_ref, groups_ref, weight_ref):
        values = ref[...].astype(F32)
        for k in range(values.shape[1]):
            info = info + jnp.where(lane == place, values[:, k : k + 1], 0.0)
            place += 1
    for h in range(2):
        for kind, ref in enumerate((tok_ref, cot_ref)):
            at = pl.ds((2 * h + kind) * tok_rows, tok_rows)
            block_ref[at, :half] = ref[:, h * half : (h + 1) * half].astype(F32)
            block_ref[at, half:] = info
    block = block_ref[...].astype(BF)
    size = block.shape[0]
    for y in range(out_ref.shape[0] // size):
        out_ref[y * size : (y + 1) * size, :] = block


def routing(info, me, top_count, limit, local_count):
    shape = (info.shape[0], 8 * local_count)
    col = iota(shape, 1)
    row = iota(shape, 0)
    target = (me * local_count + (col >> 3)).astype(F32)
    listed = jnp.zeros((info.shape[0], 1), F32)
    for j in range(limit):
        match = info[:, top_count + j : top_count + j + 1] == me.astype(F32)
        listed = jnp.maximum(listed, match.astype(F32))
    first_weight = top_count + limit
    hit = jnp.zeros(shape, F32)
    weight = jnp.zeros(shape, F32)
    picks = []
    for k in range(top_count):
        match = (info[:, k : k + 1] == target).astype(F32) * listed
        picks.append(match)
        hit = hit + match
        weight = weight + match * info[:, first_weight + k : first_weight + k + 1]
    return row, col, hit, weight, picks


def placed(hit, col):
    rows = hit.shape[0]
    earlier = (iota((rows, rows), 1) < iota((rows, rows), 0)).astype(F32).astype(BF)
    before = dot(earlier, hit.astype(BF))
    return jnp.where(before == (col & 1).astype(F32), hit, 0.0)


def dispatch_kernel(top_count, limit, local_count, me_ref, rows_ref, out_ref):
    half = out_ref.shape[1]
    info = rows_ref[:, half:].astype(F32)
    row, col, hit, weight, _ = routing(info, me_ref[0], top_count, limit, local_count)
    same = ((row >> 1) & 3) == ((col >> 1) & 3)
    place = placed(jnp.where(same, hit, 0.0), col)
    scatter = jnp.where(((col >> 1) & 1) == 1, place * weight, place).astype(BF)
    out_ref[...] = dot(scatter, rows_ref[:, :half], 0, 0).astype(BF)


def plain_order(local_count):
    size = 8 * local_count
    i = iota((size, size), 0)
    quarter = i // (2 * local_count)
    rest = i % (2 * local_count)
    where = (rest >> 1) * 8 + quarter * 2 + (rest & 1)
    return (where == iota((size, size), 1)).astype(F32).astype(BF)


def join_kernel(*refs):
    gate_up, down = refs[6:]
    part = refs[0].shape[1]
    for c in range(2):
        for kind in range(2):
            gate_up[:, pl.ds((2 * kind + c) * part, part)] = refs[3 * c + kind][...]
        down[pl.ds(c * part, part), :] = refs[3 * c + 2][...]


def expert_kernel(local_count, blocks, *refs):
    rows, outs = refs[:blocks], refs[blocks + 2 :]
    gate_up, down = refs[blocks : blocks + 2]
    slots = 2 * local_count
    half = rows[0].shape[1]
    hidden_size = down.shape[0]
    order = plain_order(local_count)
    plain = [dot(order, ref[...]).astype(BF) for ref in rows]

    def every(h, kind):
        first = (2 * h + kind) * slots
        return jnp.concatenate([block[first : first + slots] for block in plain], axis=0)

    pre = dot(every(0, 0), gate_up[:half, :]) + dot(every(1, 0), gate_up[half:, :])
    gate_pre, up_pre = pre[:, :hidden_size], pre[:, hidden_size:]
    sig = 1.0 / (1.0 + jnp.exp(-gate_pre))
    active = gate_pre * sig
    hidden = (active * up_pre).astype(BF)
    grad_hidden = dot(every(0, 1), down[:, :half], 1, 1) + dot(every(1, 1), down[:, half:], 1, 1)
    grad_gate = (grad_hidden * up_pre * sig * (1.0 + gate_pre * (1.0 - sig))).astype(BF)
    grad_up = (grad_hidden * active).astype(BF)
    grads = jnp.concatenate([grad_gate, grad_up], axis=1)
    for h in range(2):
        cols = pl.ds(h * half, half)
        for kind, value in enumerate((dot(hidden, down[:, cols]), dot(grads, gate_up[cols, :], 1, 1))):
            at = pl.ds((2 * h + kind) * slots, slots)
            for b, ref in enumerate(outs):
                ref[at, :] = value[b * slots : (b + 1) * slots].astype(ref.dtype)


def near_sum_kernel(*refs):
    refs[-1][...] = sum(ref[...].astype(F32) for ref in refs[:-1])


def total_kernel(local_count, *refs):
    total = sum(ref[...].astype(F32) for ref in refs[:-1]).astype(BF)
    refs[-1][...] = dot(plain_order(local_count), total, 0, 0).astype(BF)


def combine_kernel(top_count, limit, local_count, me_ref, rows_ref, back_ref, out_ref):
    half = back_ref.shape[1]
    info = rows_ref[:, half:].astype(F32)
    row, col, hit, weight, picks = routing(info, me_ref[0], top_count, limit, local_count)
    same = ((row >> 1) & 3) == ((col >> 1) & 3)
    place = placed(jnp.where(same, hit, 0.0), col)
    gather = jnp.where(((col >> 1) & 1) == 0, place * weight, place).astype(BF)
    out_ref[:, :half] = dot(gather, back_ref[...]).astype(BF)
    crossed = (((row >> 1) & 3) == ((col >> 1) & 3) + 1) & (((row >> 1) & 1) == 1)
    place = placed(jnp.where(crossed, hit, 0.0), col)
    pair_sum = dot(rows_ref[:, :half], back_ref[...], 1, 1) * place
    lane = iota((info.shape[0], LANES), 1)
    route = jnp.zeros((info.shape[0], LANES), F32)
    for k in range(top_count):
        value = jnp.sum(pair_sum * picks[k], axis=1, keepdims=True)
        route = route + jnp.where(lane == k, value, 0.0)
    out_ref[:, half:] = route.astype(BF)


def home_kernel(rows_ref, mixed_ref, grad_ref, route_ref, sum_ref):
    tok_rows, width = mixed_ref.shape
    half = width // 2
    size = 4 * tok_rows
    rows = rows_ref[...].astype(F32)
    total = rows[:size]
    for y in range(1, rows_ref.shape[0] // size):
        total = total + rows[y * size : (y + 1) * size]
    sum_ref[...] = total
    for h in range(2):
        cols = slice(h * half, (h + 1) * half)
        first = 2 * h * tok_rows
        mixed_ref[:, cols] = sum_ref[first : first + tok_rows, :half].astype(BF)
        grad_ref[:, cols] = sum_ref[first + tok_rows : first + 2 * tok_rows, :half].astype(BF)
    info = sum_ref[tok_rows : 2 * tok_rows, half:] + sum_ref[3 * tok_rows : 4 * tok_rows, half:]
    route_ref[...] = info[:, : route_ref.shape[1]].astype(BF)


def exchange(array, axis):
    return lax.all_to_all(array, axis, split_axis=0, concat_axis=0, tiled=True)


def after(array, earlier):
    return lax.optimization_barrier((array, earlier))[0]


def call(kernel, outs, name, *args, scratch=(), smem=0, vmem=8, flops=0):
    single = isinstance(outs, jax.ShapeDtypeStruct)
    arrays = args + ((outs,) if single else outs)
    cost = pl.CostEstimate(
        flops=flops,
        bytes_accessed=sum(a.size * a.dtype.itemsize for a in arrays),
        transcendentals=0,
    )
    return pl.pallas_call(
        kernel,
        out_shape=outs,
        in_specs=[pl.BlockSpec(memory_space=pltpu.SMEM)] * smem + [VMEM] * (len(args) - smem),
        out_specs=VMEM if single else (VMEM,) * len(outs),
        scratch_shapes=scratch,
        compiler_params=pltpu.CompilerParams(vmem_limit_bytes=vmem * MIB),
        cost_estimate=cost,
        name=name,
    )(*args)


def local(tokens, cotangent, expert_ids, node_groups, route_weight, w_gate, w_up, w_down):
    x_count = lax.axis_size("x")
    node_count = lax.axis_size("node")
    local_count = lax.axis_size("local")
    tok_rows, width = tokens.shape
    top_count = expert_ids.shape[1]
    limit = node_groups.shape[1]
    half = width // 2
    hid_part = w_gate.shape[2]
    node_rows = 4 * tok_rows * node_count
    swap = [(0, 1), (1, 0)]
    me = lax.axis_index("node").reshape(1).astype(jnp.int32)
    sizes = (top_count, limit, local_count)

    def shape(rows, cols, dtype=BF):
        return jax.ShapeDtypeStruct((rows, cols), dtype)

    slot_shape = shape(8 * local_count, half)
    node_shape = shape(node_rows, half + LANES)
    block_scratch = [pltpu.VMEM((4 * tok_rows, half + LANES), F32)]

    def turn(array, k):
        return lax.ppermute(array, "x", [(i, (i + k) % x_count) for i in range(x_count)])

    payload = call(
        payload_kernel,
        node_shape,
        "payload",
        tokens,
        cotangent,
        expert_ids,
        node_groups,
        route_weight,
        scratch=block_scratch,
        vmem=56,
    )
    gathered = exchange(payload, "node")
    send = call(
        functools.partial(dispatch_kernel, *sizes), slot_shape, "dispatch", me, gathered, smem=1, vmem=44
    )

    own = [w_gate[0], w_up[0], w_down[0]]
    joined = call(
        join_kernel,
        (shape(width, 4 * hid_part), shape(2 * hid_part, width)),
        "join",
        *own,
        *[lax.ppermute(w, "core", swap) for w in own],
        vmem=20,
    )

    mine = after(exchange(send, "local"), joined[0])

    def experts(name, dtype, *blocks):
        return call(
            functools.partial(expert_kernel, local_count, len(blocks)),
            tuple(shape(*block.shape, dtype) for block in blocks),
            name,
            *blocks,
            *joined,
            vmem=16,
            flops=12 * len(blocks) * 2 * local_count * width * 2 * hid_part,
        )

    near = sorted({1, x_count - 1})
    far = [k for k in range(1, x_count) if k not in near]
    others = {k: turn(mine, k) for k in near}
    (my_part,) = experts("mine", F32, mine)
    others.update({k: turn(after(mine, my_part), k) for k in far})
    results = {}
    last = my_part
    for name, group in (("near", near), ("far", far)):
        if group:
            first, *rest = [others[k] for k in group]
            done = experts(name, BF, after(first, last), *rest)
            last = done[0]
            results[name] = [turn(part, -k) for k, part in zip(group, done)]
    near_sum = call(
        near_sum_kernel, shape(8 * local_count, half, F32), "near_sum", my_part, *results["near"]
    )
    total = call(
        functools.partial(total_kernel, local_count),
        slot_shape,
        "total",
        near_sum,
        *results.get("far", []),
    )
    back = exchange(total, "local")
    combined = call(
        functools.partial(combine_kernel, *sizes), node_shape, "combine", me, gathered, back, smem=1
    )
    home = exchange(combined, "node")
    return call(
        home_kernel,
        (shape(tok_rows, width), shape(tok_rows, width), shape(tok_rows, top_count)),
        "home",
        home,
        scratch=block_scratch,
    )


def solution(mesh):
    shape = mesh.devices.shape
    split = Mesh(
        np.asarray(mesh.devices).reshape((shape[0] // 2, 2) + shape[1:]),
        ("x", "core", "node", "local"),
    )
    row_spec = P(("x", "core", "node", "local"), None)
    return jax.shard_map(
        local,
        mesh=split,
        in_specs=(
            row_spec,
            row_spec,
            row_spec,
            row_spec,
            row_spec,
            P(("node", "local"), None, ("x", "core")),
            P(("node", "local"), None, ("x", "core")),
            P(("node", "local"), ("x", "core"), None),
        ),
        out_specs=(row_spec, row_spec, row_spec),
        check_vma=False,
    )
```

```python
import functools

import jax
import jax.numpy as jnp
import numpy as np
from jax import lax
from jax.experimental import pallas as pl
from jax.experimental.pallas import tpu as pltpu
from jax.sharding import Mesh, PartitionSpec as P


BF = jnp.bfloat16
F32 = jnp.float32
LANES = 128
VMEM = pl.BlockSpec(memory_space=pltpu.VMEM)
MIB = 1024 * 1024


def dot(left_side, right_side, left_dim=1, right_dim=0):
    return lax.dot_general(
        left_side,
        right_side,
        (((left_dim,), (right_dim,)), ((), ())),
        preferred_element_type=F32,
    )


def iota(shape, dim):
    return lax.broadcasted_iota(jnp.int32, shape, dim)


def payload_kernel(tok_ref, cot_ref, ids_ref, groups_ref, weight_ref, out_ref, block_ref):
    tok_rows, width = tok_ref.shape
    half = width // 2
    lane = iota((tok_rows, LANES), 1)
    info = jnp.zeros((tok_rows, LANES), F32)
    place = 0
    for ref in (ids_ref, groups_ref, weight_ref):
        values = ref[...].astype(F32)
        for k in range(values.shape[1]):
            info = info + jnp.where(lane == place, values[:, k : k + 1], 0.0)
            place += 1
    for h in range(2):
        for kind, ref in enumerate((tok_ref, cot_ref)):
            at = pl.ds((2 * h + kind) * tok_rows, tok_rows)
            block_ref[at, :half] = ref[:, h * half : (h + 1) * half].astype(F32)
            block_ref[at, half:] = info
    block = block_ref[...].astype(BF)
    size = block.shape[0]
    for y in range(out_ref.shape[0] // size):
        out_ref[y * size : (y + 1) * size, :] = block


def routing(info, me, top_count, limit, local_count):
    shape = (info.shape[0], 8 * local_count)
    col = iota(shape, 1)
    row = iota(shape, 0)
    target = (me * local_count + (col >> 3)).astype(F32)
    listed = jnp.zeros((info.shape[0], 1), F32)
    for j in range(limit):
        match = info[:, top_count + j : top_count + j + 1] == me.astype(F32)
        listed = jnp.maximum(listed, match.astype(F32))
    first_weight = top_count + limit
    hit = jnp.zeros(shape, F32)
    weight = jnp.zeros(shape, F32)
    picks = []
    for k in range(top_count):
        match = (info[:, k : k + 1] == target).astype(F32) * listed
        picks.append(match)
        hit = hit + match
        weight = weight + match * info[:, first_weight + k : first_weight + k + 1]
    return row, col, hit, weight, picks


def placed(hit, col):
    rows = hit.shape[0]
    earlier = (iota((rows, rows), 1) < iota((rows, rows), 0)).astype(F32).astype(BF)
    before = dot(earlier, hit.astype(BF))
    return jnp.where(before == (col & 1).astype(F32), hit, 0.0)


def dispatch_kernel(top_count, limit, local_count, me_ref, rows_ref, out_ref):
    half = out_ref.shape[1]
    info = rows_ref[:, half:].astype(F32)
    row, col, hit, weight, _ = routing(info, me_ref[0], top_count, limit, local_count)
    same = ((row >> 1) & 3) == ((col >> 1) & 3)
    place = placed(jnp.where(same, hit, 0.0), col)
    scatter = jnp.where(((col >> 1) & 1) == 1, place * weight, place).astype(BF)
    out_ref[...] = dot(scatter, rows_ref[:, :half], 0, 0).astype(BF)


def plain_order(local_count):
    size = 8 * local_count
    i = iota((size, size), 0)
    quarter = i // (2 * local_count)
    rest = i % (2 * local_count)
    where = (rest >> 1) * 8 + quarter * 2 + (rest & 1)
    return (where == iota((size, size), 1)).astype(F32).astype(BF)


def join_kernel(*refs):
    gate_up, down = refs[6:]
    part = refs[0].shape[1]
    for c in range(2):
        for kind in range(2):
            gate_up[:, pl.ds((2 * kind + c) * part, part)] = refs[3 * c + kind][...]
        down[pl.ds(c * part, part), :] = refs[3 * c + 2][...]


def expert_kernel(local_count, blocks, *refs):
    rows, outs = refs[:blocks], refs[blocks + 2 :]
    gate_up, down = refs[blocks : blocks + 2]
    slots = 2 * local_count
    half = rows[0].shape[1]
    hidden_size = down.shape[0]
    order = plain_order(local_count)
    plain = [dot(order, ref[...]).astype(BF) for ref in rows]

    def every(h, kind):
        first = (2 * h + kind) * slots
        return jnp.concatenate([block[first : first + slots] for block in plain], axis=0)

    pre = dot(every(0, 0), gate_up[:half, :]) + dot(every(1, 0), gate_up[half:, :])
    gate_pre, up_pre = pre[:, :hidden_size], pre[:, hidden_size:]
    sig = 1.0 / (1.0 + jnp.exp(-gate_pre))
    active = gate_pre * sig
    hidden = (active * up_pre).astype(BF)
    grad_hidden = dot(every(0, 1), down[:, :half], 1, 1) + dot(every(1, 1), down[:, half:], 1, 1)
    grad_gate = (grad_hidden * up_pre * sig * (1.0 + gate_pre * (1.0 - sig))).astype(BF)
    grad_up = (grad_hidden * active).astype(BF)
    grads = jnp.concatenate([grad_gate, grad_up], axis=1)
    for h in range(2):
        cols = pl.ds(h * half, half)
        for kind, value in enumerate((dot(hidden, down[:, cols]), dot(grads, gate_up[cols, :], 1, 1))):
            at = pl.ds((2 * h + kind) * slots, slots)
            for b, ref in enumerate(outs):
                ref[at, :] = value[b * slots : (b + 1) * slots].astype(ref.dtype)


def near_sum_kernel(*refs):
    refs[-1][...] = sum(ref[...].astype(F32) for ref in refs[:-1])


def total_kernel(local_count, *refs):
    total = sum(ref[...].astype(F32) for ref in refs[:-1]).astype(BF)
    refs[-1][...] = dot(plain_order(local_count), total, 0, 0).astype(BF)


def combine_kernel(top_count, limit, local_count, me_ref, rows_ref, back_ref, out_ref):
    half = back_ref.shape[1]
    info = rows_ref[:, half:].astype(F32)
    row, col, hit, weight, picks = routing(info, me_ref[0], top_count, limit, local_count)
    same = ((row >> 1) & 3) == ((col >> 1) & 3)
    place = placed(jnp.where(same, hit, 0.0), col)
    gather = jnp.where(((col >> 1) & 1) == 0, place * weight, place).astype(BF)
    out_ref[:, :half] = dot(gather, back_ref[...]).astype(BF)
    crossed = (((row >> 1) & 3) == ((col >> 1) & 3) + 1) & (((row >> 1) & 1) == 1)
    place = placed(jnp.where(crossed, hit, 0.0), col)
    pair_sum = dot(rows_ref[:, :half], back_ref[...], 1, 1) * place
    lane = iota((info.shape[0], LANES), 1)
    route = jnp.zeros((info.shape[0], LANES), F32)
    for k in range(top_count):
        value = jnp.sum(pair_sum * picks[k], axis=1, keepdims=True)
        route = route + jnp.where(lane == k, value, 0.0)
    out_ref[:, half:] = route.astype(BF)


def home_kernel(rows_ref, mixed_ref, grad_ref, route_ref, sum_ref):
    tok_rows, width = mixed_ref.shape
    half = width // 2
    size = 4 * tok_rows
    rows = rows_ref[...].astype(F32)
    total = rows[:size]
    for y in range(1, rows_ref.shape[0] // size):
        total = total + rows[y * size : (y + 1) * size]
    sum_ref[...] = total
    for h in range(2):
        cols = slice(h * half, (h + 1) * half)
        first = 2 * h * tok_rows
        mixed_ref[:, cols] = sum_ref[first : first + tok_rows, :half].astype(BF)
        grad_ref[:, cols] = sum_ref[first + tok_rows : first + 2 * tok_rows, :half].astype(BF)
    info = sum_ref[tok_rows : 2 * tok_rows, half:] + sum_ref[3 * tok_rows : 4 * tok_rows, half:]
    route_ref[...] = info[:, : route_ref.shape[1]].astype(BF)


def exchange(array, axis):
    return lax.all_to_all(array, axis, split_axis=0, concat_axis=0, tiled=True)


def after(array, earlier):
    return lax.optimization_barrier((array, earlier))[0]


def call(kernel, outs, name, *args, scratch=(), smem=0, vmem=8, flops=0, light=False):
    single = isinstance(outs, jax.ShapeDtypeStruct)
    arrays = args + ((outs,) if single else outs)
    cost = pl.CostEstimate(
        flops=flops,
        bytes_accessed=0 if light else sum(a.size * a.dtype.itemsize for a in arrays),
        transcendentals=0,
    )
    return pl.pallas_call(
        kernel,
        out_shape=outs,
        in_specs=[pl.BlockSpec(memory_space=pltpu.SMEM)] * smem + [VMEM] * (len(args) - smem),
        out_specs=VMEM if single else (VMEM,) * len(outs),
        scratch_shapes=scratch,
        compiler_params=pltpu.CompilerParams(vmem_limit_bytes=vmem * MIB),
        cost_estimate=cost,
        name=name,
    )(*args)


def local(tokens, cotangent, expert_ids, node_groups, route_weight, w_gate, w_up, w_down):
    x_count = lax.axis_size("x")
    node_count = lax.axis_size("node")
    local_count = lax.axis_size("local")
    tok_rows, width = tokens.shape
    top_count = expert_ids.shape[1]
    limit = node_groups.shape[1]
    half = width // 2
    hid_part = w_gate.shape[2]
    node_rows = 4 * tok_rows * node_count
    swap = [(0, 1), (1, 0)]
    me = lax.axis_index("node").reshape(1).astype(jnp.int32)
    sizes = (top_count, limit, local_count)

    def shape(rows, cols, dtype=BF):
        return jax.ShapeDtypeStruct((rows, cols), dtype)

    slot_shape = shape(8 * local_count, half)
    node_shape = shape(node_rows, half + LANES)
    block_scratch = [pltpu.VMEM((4 * tok_rows, half + LANES), F32)]

    def turn(array, k):
        return lax.ppermute(array, "x", [(i, (i + k) % x_count) for i in range(x_count)])

    payload = call(
        payload_kernel,
        node_shape,
        "payload",
        tokens,
        cotangent,
        expert_ids,
        node_groups,
        route_weight,
        scratch=block_scratch,
        vmem=56,
    )
    gathered = exchange(payload, "node")
    send = call(
        functools.partial(dispatch_kernel, *sizes), slot_shape, "dispatch", me, gathered, smem=1, vmem=44
    )

    own = [w_gate[0], w_up[0], w_down[0]]
    joined = call(
        join_kernel,
        (shape(width, 4 * hid_part), shape(2 * hid_part, width)),
        "join",
        *own,
        *[lax.ppermute(w, "core", swap) for w in own],
        vmem=20,
    )

    mine = after(exchange(send, "local"), joined[0])

    def experts(name, dtype, *blocks, light=False):
        return call(
            functools.partial(expert_kernel, local_count, len(blocks)),
            tuple(shape(*block.shape, dtype) for block in blocks),
            name,
            *blocks,
            *joined,
            vmem=16,
            flops=0 if light else 12 * len(blocks) * 2 * local_count * width * 2 * hid_part,
            light=light,
        )

    near = sorted({1, x_count - 1})
    far = [k for k in range(1, x_count) if k not in near]
    others = {k: turn(mine, k) for k in near}
    (my_part,) = experts("mine", F32, mine)
    others.update({k: turn(after(mine, my_part), k) for k in far})
    results = {}
    last = my_part
    for name, group in (("near", near), ("far", far)):
        if group:
            first, *rest = [others[k] for k in group]
            done = experts(name, BF, after(first, last), *rest, light=name == "far")
            last = done[0]
            results[name] = [turn(part, -k) for k, part in zip(group, done)]
    near_sum = call(
        near_sum_kernel,
        shape(8 * local_count, half, F32),
        "near_sum",
        my_part,
        *results["near"],
        flops=4 * 10**9,
    )
    total = call(
        functools.partial(total_kernel, local_count),
        slot_shape,
        "total",
        near_sum,
        *results.get("far", []),
    )
    back = exchange(total, "local")
    combined = call(
        functools.partial(combine_kernel, *sizes), node_shape, "combine", me, gathered, back, smem=1
    )
    home = exchange(combined, "node")
    return call(
        home_kernel,
        (shape(tok_rows, width), shape(tok_rows, width), shape(tok_rows, top_count)),
        "home",
        home,
        scratch=block_scratch,
    )


def solution(mesh):
    shape = mesh.devices.shape
    split = Mesh(
        np.asarray(mesh.devices).reshape((shape[0] // 2, 2) + shape[1:]),
        ("x", "core", "node", "local"),
    )
    row_spec = P(("x", "core", "node", "local"), None)
    return jax.shard_map(
        local,
        mesh=split,
        in_specs=(
            row_spec,
            row_spec,
            row_spec,
            row_spec,
            row_spec,
            P(("node", "local"), None, ("x", "core")),
            P(("node", "local"), None, ("x", "core")),
            P(("node", "local"), ("x", "core"), None),
        ),
        out_specs=(row_spec, row_spec, row_spec),
        check_vma=False,
    )
```

```python
import functools

import jax
import jax.numpy as jnp
import numpy as np
from jax import lax
from jax.experimental import pallas as pl
from jax.experimental.pallas import tpu as pltpu
from jax.sharding import Mesh, PartitionSpec as P


BF = jnp.bfloat16
F32 = jnp.float32
LANES = 128
VMEM = pl.BlockSpec(memory_space=pltpu.VMEM)
MIB = 1024 * 1024


def dot(left_side, right_side, left_dim=1, right_dim=0):
    return lax.dot_general(
        left_side,
        right_side,
        (((left_dim,), (right_dim,)), ((), ())),
        preferred_element_type=F32,
    )


def iota(shape, dim):
    return lax.broadcasted_iota(jnp.int32, shape, dim)


def payload_kernel(tok_ref, cot_ref, ids_ref, groups_ref, weight_ref, out_ref, block_ref):
    tok_rows, width = tok_ref.shape
    half = width // 2
    lane = iota((tok_rows, LANES), 1)
    info = jnp.zeros((tok_rows, LANES), F32)
    place = 0
    for ref in (ids_ref, groups_ref, weight_ref):
        values = ref[...].astype(F32)
        for k in range(values.shape[1]):
            info = info + jnp.where(lane == place, values[:, k : k + 1], 0.0)
            place += 1
    for h in range(2):
        for kind, ref in enumerate((tok_ref, cot_ref)):
            at = pl.ds((2 * h + kind) * tok_rows, tok_rows)
            block_ref[at, :half] = ref[:, h * half : (h + 1) * half].astype(F32)
            block_ref[at, half:] = info
    block = block_ref[...].astype(BF)
    size = block.shape[0]
    for y in range(out_ref.shape[0] // size):
        out_ref[y * size : (y + 1) * size, :] = block


def routing(info, me, top_count, limit, local_count):
    shape = (info.shape[0], 8 * local_count)
    col = iota(shape, 1)
    row = iota(shape, 0)
    target = (me * local_count + (col >> 3)).astype(F32)
    listed = jnp.zeros((info.shape[0], 1), F32)
    for j in range(limit):
        match = info[:, top_count + j : top_count + j + 1] == me.astype(F32)
        listed = jnp.maximum(listed, match.astype(F32))
    first_weight = top_count + limit
    hit = jnp.zeros(shape, F32)
    weight = jnp.zeros(shape, F32)
    picks = []
    for k in range(top_count):
        match = (info[:, k : k + 1] == target).astype(F32) * listed
        picks.append(match)
        hit = hit + match
        weight = weight + match * info[:, first_weight + k : first_weight + k + 1]
    return row, col, hit, weight, picks


def placed(hit, col):
    rows = hit.shape[0]
    earlier = (iota((rows, rows), 1) < iota((rows, rows), 0)).astype(F32).astype(BF)
    before = dot(earlier, hit.astype(BF))
    return jnp.where(before == (col & 1).astype(F32), hit, 0.0)


def dispatch_kernel(top_count, limit, local_count, me_ref, rows_ref, out_ref):
    half = out_ref.shape[1]
    info = rows_ref[:, half:].astype(F32)
    row, col, hit, weight, _ = routing(info, me_ref[0], top_count, limit, local_count)
    same = ((row >> 1) & 3) == ((col >> 1) & 3)
    place = placed(jnp.where(same, hit, 0.0), col)
    scatter = jnp.where(((col >> 1) & 1) == 1, place * weight, place).astype(BF)
    out_ref[...] = dot(scatter, rows_ref[:, :half], 0, 0).astype(BF)


def plain_order(local_count):
    size = 8 * local_count
    i = iota((size, size), 0)
    quarter = i // (2 * local_count)
    rest = i % (2 * local_count)
    where = (rest >> 1) * 8 + quarter * 2 + (rest & 1)
    return (where == iota((size, size), 1)).astype(F32).astype(BF)


def join_kernel(*refs):
    gate_up, down = refs[6:8], refs[8:10]
    part = refs[0].shape[1]
    half = gate_up[0].shape[0]
    for h in range(2):
        at = pl.ds(h * half, half)
        for c in range(2):
            for kind in range(2):
                gate_up[h][:, pl.ds((2 * kind + c) * part, part)] = refs[3 * c + kind][at, :]
            down[h][pl.ds(c * part, part), :] = refs[3 * c + 2][:, at]


def expert_kernel(local_count, blocks, *refs):
    rows, outs = refs[:blocks], refs[blocks + 4 :]
    gate_up, down = refs[blocks : blocks + 2], refs[blocks + 2 : blocks + 4]
    slots = 2 * local_count
    half = rows[0].shape[1]
    hidden_size = down[0].shape[0]
    order = plain_order(local_count)
    plain = [dot(order, ref[...]).astype(BF) for ref in rows]

    def every(h, kind):
        first = (2 * h + kind) * slots
        return jnp.concatenate([block[first : first + slots] for block in plain], axis=0)

    pre = dot(every(0, 0), gate_up[0][...]) + dot(every(1, 0), gate_up[1][...])
    gate_pre, up_pre = pre[:, :hidden_size], pre[:, hidden_size:]
    sig = 1.0 / (1.0 + jnp.exp(-gate_pre))
    active = gate_pre * sig
    hidden = (active * up_pre).astype(BF)
    grad_hidden = dot(every(0, 1), down[0][...], 1, 1) + dot(every(1, 1), down[1][...], 1, 1)
    grad_gate = (grad_hidden * up_pre * sig * (1.0 + gate_pre * (1.0 - sig))).astype(BF)
    grad_up = (grad_hidden * active).astype(BF)
    grads = jnp.concatenate([grad_gate, grad_up], axis=1)
    for h in range(2):
        for kind, value in enumerate((dot(hidden, down[h][...]), dot(grads, gate_up[h][...], 1, 1))):
            at = pl.ds((2 * h + kind) * slots, slots)
            for b, ref in enumerate(outs):
                ref[at, :] = value[b * slots : (b + 1) * slots].astype(ref.dtype)


def near_sum_kernel(*refs):
    refs[-1][...] = sum(ref[...].astype(F32) for ref in refs[:-1])


def total_kernel(local_count, *refs):
    total = sum(ref[...].astype(F32) for ref in refs[:-1]).astype(BF)
    refs[-1][...] = dot(plain_order(local_count), total, 0, 0).astype(BF)


def combine_kernel(top_count, limit, local_count, me_ref, rows_ref, back_ref, out_ref):
    half = back_ref.shape[1]
    info = rows_ref[:, half:].astype(F32)
    row, col, hit, weight, picks = routing(info, me_ref[0], top_count, limit, local_count)
    same = ((row >> 1) & 3) == ((col >> 1) & 3)
    place = placed(jnp.where(same, hit, 0.0), col)
    gather = jnp.where(((col >> 1) & 1) == 0, place * weight, place).astype(BF)
    out_ref[:, :half] = dot(gather, back_ref[...]).astype(BF)
    crossed = (((row >> 1) & 3) == ((col >> 1) & 3) + 1) & (((row >> 1) & 1) == 1)
    place = placed(jnp.where(crossed, hit, 0.0), col)
    pair_sum = dot(rows_ref[:, :half], back_ref[...], 1, 1) * place
    lane = iota((info.shape[0], LANES), 1)
    route = jnp.zeros((info.shape[0], LANES), F32)
    for k in range(top_count):
        value = jnp.sum(pair_sum * picks[k], axis=1, keepdims=True)
        route = route + jnp.where(lane == k, value, 0.0)
    out_ref[:, half:] = route.astype(BF)


def home_kernel(rows_ref, mixed_ref, grad_ref, route_ref, sum_ref):
    tok_rows, width = mixed_ref.shape
    half = width // 2
    size = 4 * tok_rows
    rows = rows_ref[...].astype(F32)
    total = rows[:size]
    for y in range(1, rows_ref.shape[0] // size):
        total = total + rows[y * size : (y + 1) * size]
    sum_ref[...] = total
    for h in range(2):
        cols = slice(h * half, (h + 1) * half)
        first = 2 * h * tok_rows
        mixed_ref[:, cols] = sum_ref[first : first + tok_rows, :half].astype(BF)
        grad_ref[:, cols] = sum_ref[first + tok_rows : first + 2 * tok_rows, :half].astype(BF)
    info = sum_ref[tok_rows : 2 * tok_rows, half:] + sum_ref[3 * tok_rows : 4 * tok_rows, half:]
    route_ref[...] = info[:, : route_ref.shape[1]].astype(BF)


def exchange(array, axis):
    return lax.all_to_all(array, axis, split_axis=0, concat_axis=0, tiled=True)


def after(array, earlier):
    return lax.optimization_barrier((array, earlier))[0]


def call(kernel, outs, name, *args, scratch=(), smem=0, vmem=8, flops=0, light=False):
    single = isinstance(outs, jax.ShapeDtypeStruct)
    arrays = args + ((outs,) if single else outs)
    cost = pl.CostEstimate(
        flops=flops,
        bytes_accessed=0 if light else sum(a.size * a.dtype.itemsize for a in arrays),
        transcendentals=0,
    )
    return pl.pallas_call(
        kernel,
        out_shape=outs,
        in_specs=[pl.BlockSpec(memory_space=pltpu.SMEM)] * smem + [VMEM] * (len(args) - smem),
        out_specs=VMEM if single else (VMEM,) * len(outs),
        scratch_shapes=scratch,
        compiler_params=pltpu.CompilerParams(vmem_limit_bytes=vmem * MIB),
        cost_estimate=cost,
        name=name,
    )(*args)


def local(tokens, cotangent, expert_ids, node_groups, route_weight, w_gate, w_up, w_down):
    x_count = lax.axis_size("x")
    node_count = lax.axis_size("node")
    local_count = lax.axis_size("local")
    tok_rows, width = tokens.shape
    top_count = expert_ids.shape[1]
    limit = node_groups.shape[1]
    half = width // 2
    hid_part = w_gate.shape[2]
    node_rows = 4 * tok_rows * node_count
    swap = [(0, 1), (1, 0)]
    me = lax.axis_index("node").reshape(1).astype(jnp.int32)
    sizes = (top_count, limit, local_count)

    def shape(rows, cols, dtype=BF):
        return jax.ShapeDtypeStruct((rows, cols), dtype)

    slot_shape = shape(8 * local_count, half)
    node_shape = shape(node_rows, half + LANES)
    block_scratch = [pltpu.VMEM((4 * tok_rows, half + LANES), F32)]

    def turn(array, k):
        return lax.ppermute(array, "x", [(i, (i + k) % x_count) for i in range(x_count)])

    payload = call(
        payload_kernel,
        node_shape,
        "payload",
        tokens,
        cotangent,
        expert_ids,
        node_groups,
        route_weight,
        scratch=block_scratch,
        vmem=56,
    )
    gathered = exchange(payload, "node")
    send = call(
        functools.partial(dispatch_kernel, *sizes), slot_shape, "dispatch", me, gathered, smem=1, vmem=44
    )

    own = [w_gate[0], w_up[0], w_down[0]]
    joined = call(
        join_kernel,
        (shape(half, 4 * hid_part),) * 2 + (shape(2 * hid_part, half),) * 2,
        "join",
        *own,
        *[lax.ppermute(w, "core", swap) for w in own],
        vmem=20,
    )

    mine = after(exchange(send, "local"), joined[0])

    def experts(name, dtype, *blocks, light=False):
        return call(
            functools.partial(expert_kernel, local_count, len(blocks)),
            tuple(shape(*block.shape, dtype) for block in blocks),
            name,
            *blocks,
            *joined,
            vmem=16,
            flops=0 if light else 12 * len(blocks) * 2 * local_count * width * 2 * hid_part,
            light=light,
        )

    near = sorted({1, x_count - 1})
    far = [k for k in range(1, x_count) if k not in near]
    others = {k: turn(mine, k) for k in near}
    (my_part,) = experts("mine", F32, mine)
    others.update({k: turn(after(mine, my_part), k) for k in far})
    results = {}
    last = my_part
    for name, group in (("near", near), ("far", far)):
        if group:
            first, *rest = [others[k] for k in group]
            done = experts(name, BF, after(first, last), *rest, light=name == "far")
            last = done[0]
            results[name] = [turn(part, -k) for k, part in zip(group, done)]
    near_sum = call(
        near_sum_kernel,
        shape(8 * local_count, half, F32),
        "near_sum",
        my_part,
        *results["near"],
        flops=4 * 10**9,
    )
    total = call(
        functools.partial(total_kernel, local_count),
        slot_shape,
        "total",
        near_sum,
        *results.get("far", []),
    )
    back = exchange(total, "local")
    combined = call(
        functools.partial(combine_kernel, *sizes), node_shape, "combine", me, gathered, back, smem=1
    )
    home = exchange(combined, "node")
    return call(
        home_kernel,
        (shape(tok_rows, width), shape(tok_rows, width), shape(tok_rows, top_count)),
        "home",
        home,
        scratch=block_scratch,
    )


def solution(mesh):
    shape = mesh.devices.shape
    split = Mesh(
        np.asarray(mesh.devices).reshape((shape[0] // 2, 2) + shape[1:]),
        ("x", "core", "node", "local"),
    )
    row_spec = P(("x", "core", "node", "local"), None)
    return jax.shard_map(
        local,
        mesh=split,
        in_specs=(
            row_spec,
            row_spec,
            row_spec,
            row_spec,
            row_spec,
            P(("node", "local"), None, ("x", "core")),
            P(("node", "local"), None, ("x", "core")),
            P(("node", "local"), ("x", "core"), None),
        ),
        out_specs=(row_spec, row_spec, row_spec),
        check_vma=False,
    )
```
